32 devices in a mesh: gx: 8 (over z, y), gy: 4 (over x, core).
Axes of the slice: x: 2, y: 2, z: 4, core: 2. Of those that a mesh axis runs over, the one named last changes fastest.
Arguments:
- jitter: float32 [4096, 3, 128], P(('gx', 'gy')), may hold values from -0.2 to 0.2
- displacement: float32 [4096, 3, 128], P(('gx', 'gy')), may hold values from -0.1 to 0.1
- modulus: float32 [4096, 128], P(('gx', 'gy')), may hold values from 0.1 to 1
- start_vec: float32 [4096, 3, 128], P(('gx', 'gy')), may hold values from -6 to 6
- old_home: int32 [4096], P(('gx', 'gy')), may hold values from 0 to 4095, as said below
- ghost_send: int32 [32, 9, 16], P(('gx', 'gy')), may hold values from -1 to 127, as said below
- pair_list: int32 [32, 4, 512], P(('gx', 'gy')), may hold values from -1 to 271, as said below
- pair_count: int32 [32], P(('gx', 'gy')), may hold values from 64 to 512, as said below
- broken: int32 [16384, 16, 128], P(('gx', 'gy')), may hold values from 0 to 255
Outputs:
- first_image: float32 [4096, 3, 128], P(('gx', 'gy'))
- second_image: float32 [4096, 3, 128], P(('gx', 'gy'))
The draws below stay inside these ranges and needn't reach their ends.
Inputs may be any that keep to these rules, and one draw needn't show every extreme that they name: `old_home`: A permutation. Row i of the old layout and row j of the rebalanced layout belong to devices i // 128 and j // 128; each device hands exactly 16 of its old tiles to each device beside it along gx or along gy (grid places differing by one in one coordinate, no wrap) and keeps the others. `ghost_send`: directions whose receiver lies outside the grid, and direction 4, hold only -1; for every other direction the first 1 to 16 slots hold rows below 128 and the rest -1; every device fills all 16 slots toward some neighbour along gx or gy. `pair_list`: tile is below 128; partner is below 128, or 128 + e * 16 + k where the device at offset (e // 3 - 1, e mod 3 - 1) exists and its slot k toward this device holds a row; shifts are -1, 0 or 1; when both shifts are 0, partner equals tile. Slots past the count are filled the same way. `pair_count`: at least 64; some device has 512.
All inputs are finite; a program needn't handle non-finite values.
Results may differ from the reference program's by a relative error of at most 0.0003.
Values sent between devices are 32-bit elements; how exact they have to be, the bound alone decides.
A program may use at most 64 MiB of HBM per device.

```python
import math
import jax
import jax.numpy as jnp
from jax import lax

P_SIZE = 128
TILES_DEV = 128
GCAP = 16
CAP = 16
TILES = 4096
PAIRS = 512
WORDS = 16
N_GX = 8
N_GY = 4
DEVICES = 32


def grid_valid():
    device_count = TILES // TILES_DEV
    device_ids = jnp.arange(device_count)
    place_x = device_ids // N_GY
    place_y = device_ids % N_GY
    cells = jnp.arange(9)
    near_x = place_x[:, None] + cells[None, :] // 3 - 1
    near_y = place_y[:, None] + cells[None, :] % 3 - 1
    inside = (near_x >= 0) & (near_x < N_GX) & (near_y >= 0) & (near_y < N_GY)
    return inside & (cells[None, :] != 4)


def ghost_counts(key):
    device_count = TILES // TILES_DEV
    key_count, key_coin = jax.random.split(jax.random.fold_in(key, 11))
    counts = jax.random.randint(key_count, (device_count, 9), 1, GCAP + 1)
    device_ids = jnp.arange(device_count)
    place_x = device_ids // N_GY
    place_y = device_ids % N_GY
    step_x = jnp.where(place_x < N_GX - 1, 1, -1)
    step_y = jnp.where(place_y < N_GY - 1, 1, -1)
    coin = jax.random.randint(key_coin, (device_count,), 0, 2)
    full_cell = jnp.where(coin == 0, (1 + step_x) * 3 + 1, 3 + (1 + step_y))
    counts = counts.at[device_ids, full_cell].set(GCAP)
    return jnp.where(grid_valid(), counts, 0)


def draw_ghost_send(key, part):
    device_count = TILES // TILES_DEV
    counts = ghost_counts(key)
    rows_drawn = jax.random.randint(jax.random.fold_in(key, 12), (device_count, 9, GCAP), 0, TILES_DEV)
    slot_index = jnp.arange(GCAP)
    return jnp.where(slot_index[None, None, :] < counts[:, :, None], rows_drawn, -1).astype(jnp.int32)


def draw_pair_list(key, part):
    device_count = TILES // TILES_DEV
    counts = ghost_counts(key)
    keys_all = jax.random.split(jax.random.fold_in(key, 13), 6)
    tile_row = jax.random.randint(keys_all[0], (device_count, PAIRS), 0, TILES_DEV)
    local_row = jax.random.randint(keys_all[1], (device_count, PAIRS), 0, TILES_DEV)
    drawn_dir = jax.random.randint(keys_all[2], (device_count, PAIRS), 0, 8)
    cell = drawn_dir + (drawn_dir >= 4).astype(jnp.int32)
    off_x = cell // 3 - 1
    off_y = cell % 3 - 1
    device_ids = jnp.arange(device_count)[:, None]
    near_x = device_ids // N_GY + off_x
    near_y = device_ids % N_GY + off_y
    exists = (near_x >= 0) & (near_x < N_GX) & (near_y >= 0) & (near_y < N_GY)
    source = jnp.clip(near_x * N_GY + near_y, 0, device_count - 1)
    limit = jnp.where(exists, counts[source, (1 - off_x) * 3 + (1 - off_y)], 0)
    slot_drawn = jax.random.randint(keys_all[3], (device_count, PAIRS), 0, jnp.maximum(limit, 1))
    ghost_ref = TILES_DEV + cell * GCAP + slot_drawn
    choose_kind = jax.random.randint(keys_all[4], (device_count, PAIRS), 0, 2)
    partner = jnp.where((choose_kind == 1) & (limit > 0), ghost_ref, local_row)
    shifts = jax.random.randint(keys_all[5], (device_count, 2, PAIRS), -1, 2)
    coincide = jnp.logical_and(shifts[:, 0] == 0, shifts[:, 1] == 0)
    partner = jnp.where(coincide, tile_row, partner)
    return jnp.stack([tile_row, partner, shifts[:, 0], shifts[:, 1]], axis=1).astype(jnp.int32)


def draw_pair_count(key, part):
    device_count = TILES // TILES_DEV
    key_level, key_top = jax.random.split(jax.random.fold_in(key, 14))
    level = jax.random.randint(key_level, (device_count,), 0, 65)
    level = level.at[jax.random.randint(key_top, (), 0, device_count)].set(64)
    return (PAIRS // 8 + (PAIRS - PAIRS // 8) * level * level // 4096).astype(jnp.int32)


def draw_old_home(key, part):
    device_count = TILES // TILES_DEV
    keys_all = jax.random.split(jax.random.fold_in(key, 15), 2)
    shuffles = jax.vmap(lambda sub_key: jax.random.permutation(sub_key, TILES_DEV))(jax.random.split(keys_all[0], device_count))
    block = jnp.minimum(shuffles // CAP, 4)
    step_x = jnp.array([-1, 1, 0, 0, 0])[block]
    step_y = jnp.array([0, 0, -1, 1, 0])[block]
    device_ids = jnp.arange(device_count)[:, None]
    near_x = device_ids // N_GY + step_x
    near_y = device_ids % N_GY + step_y
    exists = (block < 4) & (near_x >= 0) & (near_x < N_GX) & (near_y >= 0) & (near_y < N_GY)
    target = jnp.where(exists, near_x * N_GY + near_y, device_ids).reshape(-1)
    order_key = target * TILES + jax.random.permutation(keys_all[1], TILES)
    return jnp.argsort(order_key, stable=True).astype(jnp.int32)


def place_ends(values, rng, low, top_value):
    extent = values.shape
    place = [jax.random.randint(jax.random.fold_in(rng, axis), (), 0, extent[axis]) for axis in range(len(extent))]
    values = values.at[tuple(place)].set(low)
    longest = extent.index(max(extent))
    place[longest] = (place[longest] + 1) % extent[longest]
    return values.at[tuple(place)].set(top_value)


def steps_of(rng, extent, pieces, low, top_value):
    def one(axis_at, shards_of):
        steps = jax.random.uniform(jax.random.fold_in(jax.random.fold_in(rng, 6), axis_at), (shards_of,), jnp.float32, low / len(pieces), top_value / len(pieces))
        return jnp.repeat(jnp.exp(steps), extent[axis_at] // shards_of).reshape((-1,) + (1,) * (len(extent) - axis_at - 1))

    gain = one(*pieces[0])
    for cut in pieces[1:]:
        gain = gain * one(*cut)
    return gain


def centred(key, dims, scale, reach, shards=(), kind=jnp.bfloat16):
    values = jax.random.normal(key, dims, jnp.float32) * scale
    if len(shards) > 0:
        values = steps_of(key, dims, shards, -0.22, 0.18) * values
    return jnp.clip(values, min=-reach, max=reach).astype(kind)


def setup_inputs(seed: int = 0) -> dict:
    keys = jax.random.split(jax.random.key(seed), 10)
    jitter = jnp.clip(jax.random.uniform(keys[0], (TILES, 3, P_SIZE), jnp.float32, -0.2, 0.2) * steps_of(keys[0], (TILES, 3, P_SIZE), ((0, 32),), -0.4, 0.0), -0.2, 0.2)
    displacement = jnp.clip(jax.random.uniform(keys[1], (TILES, 3, P_SIZE), jnp.float32, -0.1, 0.1) * steps_of(keys[1], (TILES, 3, P_SIZE), ((0, 32),), -0.4, 0.0), -0.1, 0.1)
    modulus = jnp.clip(jnp.exp(math.log(1.0) - 2.3025851 * jax.random.uniform(keys[2], (TILES, P_SIZE), jnp.float32) ** steps_of(keys[2], (TILES, P_SIZE), ((0, 32),), -0.2, 0.2)), 0.1, 1.0)
    start_vec = centred(keys[3], (TILES, 3, P_SIZE), 1.0, 6.0, ((0, 32),), jnp.float32)
    old_home = draw_old_home(jax.random.fold_in(keys[9], 71), 0)
    ghost_send = draw_ghost_send(jax.random.fold_in(keys[9], 71), 0)
    pair_list = draw_pair_list(jax.random.fold_in(keys[9], 71), 0)
    pair_count = draw_pair_count(jax.random.fold_in(keys[9], 71), 0)
    broken = place_ends(jax.random.randint(keys[8], (DEVICES * PAIRS, WORDS, P_SIZE), 0, 256), jax.random.fold_in(keys[8], 1), 0, 255).astype(jnp.int32)
    return {"jitter": jitter, "displacement": displacement, "modulus": modulus, "start_vec": start_vec, "old_home": old_home, "ghost_send": ghost_send, "pair_list": pair_list, "pair_count": pair_count, "broken": broken}


def lattice(points):
    counter = jnp.arange(points, dtype=jnp.int32)
    return jnp.stack([counter % 8, counter // 8 % (points // 16), counter // (points // 2)]).astype(jnp.float32)

def pair_force(geom_a, geom_b, vector_a, vector_b, shifts, flag_words):
    placed_a, current_a, modulus_a = geom_a
    placed_b, current_b, modulus_b = geom_b
    points = placed_a.shape[1]
    offset = jnp.stack([shifts[0] * 8, shifts[1] * (points // 16), shifts[0] * 0]).astype(jnp.float32)
    coincide = jnp.logical_and(shifts[0] == 0, shifts[1] == 0)
    diagonal = jnp.where(coincide, jnp.eye(points, dtype=jnp.float32), jnp.zeros((points, points), jnp.float32))
    ref_bond = placed_b[:, :, None] + offset[:, None, None] - placed_a[:, None, :]
    cur_bond = ref_bond + current_b[:, :, None] - current_a[:, None, :]
    ref_square = lax.optimization_barrier(jnp.sum(ref_bond * ref_bond, axis=0)) + diagonal
    cur_square = lax.optimization_barrier(jnp.sum(cur_bond * cur_bond, axis=0)) + diagonal
    ref_len = jnp.sqrt(ref_square)
    cur_len = jnp.sqrt(cur_square)
    flag_bits = jnp.right_shift(flag_words[:, None, :], jnp.arange(8, dtype=jnp.int32)[None, :, None]) & 1
    intact = 1.0 - flag_bits.reshape(points, points).astype(jnp.float32)
    weight = jnp.maximum(1.0 - ref_square / 9.0, 0.0) * intact * (1.0 - diagonal)
    bond_scale = 0.05 * (modulus_b[:, None] + modulus_a[None, :]) * weight
    stiff_axial = bond_scale / ref_len
    stiff_cross = bond_scale * (cur_len - ref_len) / (ref_len * cur_len)
    direction = cur_bond / cur_len
    change = vector_b[:, :, None] - vector_a[:, None, :]
    projected = lax.optimization_barrier(jnp.sum(direction * change, axis=0))
    return lax.optimization_barrier(jnp.sum(stiff_cross * change + (stiff_axial - stiff_cross) * direction * projected, axis=1))

def reference(jitter, displacement, modulus, start_vec, old_home, ghost_send, pair_list, pair_count, broken):
    device_count = TILES // TILES_DEV
    placed = lattice(P_SIZE)[None] + jitter[old_home]
    current = displacement[old_home]
    moduli = modulus[old_home]
    vector = start_vec[old_home]
    owner = jnp.broadcast_to(jnp.arange(device_count, dtype=jnp.int32)[:, None], (device_count, PAIRS))
    grid_x = owner // N_GY
    grid_y = owner % N_GY
    tile_row = pair_list[:, 0]
    partner = pair_list[:, 1]
    ghost_ref = jnp.maximum(partner - TILES_DEV, 0)
    direction_in = ghost_ref // GCAP
    ghost_slot = ghost_ref % GCAP
    off_x = direction_in // 3 - 1
    off_y = direction_in % 3 - 1
    source = jnp.clip((grid_x + off_x) * N_GY + (grid_y + off_y), 0, device_count - 1).astype(jnp.int32)
    send_dir = ((1 - off_x) * 3 + (1 - off_y)).astype(jnp.int32)
    remote = ghost_send[source, send_dir, ghost_slot]
    row_b = jnp.where(partner < TILES_DEV, owner * TILES_DEV + partner, source * TILES_DEV + remote).reshape(-1).astype(jnp.int32)
    row_a = (owner * TILES_DEV + tile_row).reshape(-1).astype(jnp.int32)
    shifts = jnp.transpose(pair_list[:, 2:4], (0, 2, 1)).reshape(-1, 2)
    active = (jnp.arange(PAIRS, dtype=jnp.int32)[None, :] < pair_count[:, None]).reshape(-1).astype(jnp.float32)
    group_len = 64

    def tangent_apply(field):

        def pair_group(batch):
            rows_a, rows_b, group_shifts, group_words = batch
            geom_a = (placed[rows_a], current[rows_a], moduli[rows_a])
            geom_b = (placed[rows_b], current[rows_b], moduli[rows_b])
            return jax.vmap(pair_force)(geom_a, geom_b, field[rows_a], field[rows_b], group_shifts, group_words)
        pair_terms = lax.map(pair_group, (row_a.reshape(-1, group_len), row_b.reshape(-1, group_len), shifts.reshape(-1, group_len, 2), broken.reshape(-1, group_len, WORDS, P_SIZE)))
        pair_terms = pair_terms.reshape(-1, 3, P_SIZE) * active[:, None, None]
        return jax.ops.segment_sum(pair_terms, row_a, num_segments=TILES)
    first_image = tangent_apply(vector)
    second_image = tangent_apply(first_image)
    return (first_image, second_image)
```

```python
import functools
import jax
import jax.numpy as jnp
from jax import lax
from jax.experimental import pallas as pl
from jax.experimental.pallas import tpu as pltpu
from jax.sharding import PartitionSpec as P

CAP = 16
F32 = jnp.float32
VMEM = pl.BlockSpec(memory_space=pltpu.VMEM)
SMEM = pl.BlockSpec(memory_space=pltpu.SMEM)
LIMIT = pltpu.CompilerParams(vmem_limit_bytes=48 * 1024 * 1024)
DIRS = (0, 1, 2, 3, 5, 6, 7, 8)


def lattice(points):
    counter = jnp.arange(points, dtype=jnp.int32)
    return jnp.stack([counter % 8, counter // 8 % (points // 16), counter // (points // 2)]).astype(F32)


def hand_kernel(asked, jit, disp, mod, vec, *outs):
    for out in outs:
        out[...] = jnp.zeros_like(out)

    def body(i, carry):
        for d, out in enumerate(outs):
            row = asked[d, i]
            out[i, 0:3] = jit[row]
            out[i, 3:6] = disp[row]
            out[i, 6:7] = mod[pl.ds(row, 1)]
            out[i, 8:11] = vec[row]
        return carry

    lax.fori_loop(0, CAP, body, 0)


def settle_kernel(pick, send, lat8, jit, disp, mod, vec, in0, in1, in2, in3, local, *rest):
    outs, pool = rest[:8], rest[8]
    rows = jit.shape[0]
    pool[0:rows] = jnp.zeros((rows,) + pool.shape[1:], F32)
    pool[0:rows, 0:3, :] = jit[...]
    pool[0:rows, 3:6, :] = disp[...]
    pool[0:rows, 8:11, :] = vec[...]

    def put_mod(j, carry):
        pool[j, 6:7, :] = mod[pl.ds(j, 1)]
        return carry

    lax.fori_loop(0, rows, put_mod, 0, unroll=8)
    for d, arrived in enumerate((in0, in1, in2, in3)):
        pool[rows + d * CAP : rows + (d + 1) * CAP] = arrived[...]
    points = jit.shape[2]
    sub = lax.broadcasted_iota(jnp.int32, (8, points), 0)
    scale = jnp.where(sub == 6, 0.05, 1.0)
    moved = (sub >= 3) & (sub < 6)

    def settle(j, carry):
        held = pool[pick[j]]
        low = held[0:8]
        base = low + lat8[...]
        shifted = jnp.where(moved, pltpu.roll(base, 3, 0), 0.0)
        local[j, 0:8] = low * scale + jnp.where(moved, 0.0, lat8[...]) + shifted
        local[j, 8:16] = held[8:16]
        return carry

    lax.fori_loop(0, rows, settle, 0, unroll=8)

    def ghosts(i, carry):
        for c, out in zip(DIRS, outs):
            out[i] = local[jnp.maximum(send[c, i], 0)]
        return carry

    lax.fori_loop(0, outs[0].shape[0], ghosts, 0)


def apply_kernel(first, pairs, count, send, words, local, *rest):
    ghosts, rest = rest[:8], rest[8:]
    if not first:
        field, field_ghosts, rest = rest[0], rest[1:9], rest[9:]
    image, rest = rest[0], rest[1:]
    if first:
        sends, rest = rest[:8], rest[8:]
    full, turned, total = rest
    rows, _, points = local.shape
    cap = ghosts[0].shape[0]
    full[0:rows] = local[...]
    full[rows + 4 * cap : rows + 5 * cap] = jnp.zeros((cap,) + full.shape[1:], F32)
    for e, ghost in zip(DIRS, ghosts):
        full[rows + e * cap : rows + (e + 1) * cap] = ghost[...]
    if not first:
        full[0:rows, 8:11, :] = field[...]
        for e, ghost in zip(DIRS, field_ghosts):
            full[rows + e * cap : rows + (e + 1) * cap, 8:16, :] = ghost[...]

    def turn(j, carry):
        turned[j] = jnp.transpose(full[j])
        return carry

    lax.fori_loop(0, full.shape[0], turn, 0, unroll=8)
    total[...] = jnp.zeros_like(total)

    def bonds(side_b, side_a, flags, acc, guard):
        part = lambda c: side_b[:, c : c + 1]
        xi = [part(c) - side_a[c] for c in range(3)]
        y = [part(3 + c) - side_a[3 + c] for c in range(3)]
        dv = [part(8 + c) - side_a[8 + c] for c in range(3)]
        r2 = xi[0] * xi[0] + xi[1] * xi[1] + xi[2] * xi[2]
        l2 = y[0] * y[0] + y[1] * y[1] + y[2] * y[2]
        weight = jnp.maximum(1.0 - r2 * (1.0 / 9.0), 0.0)
        c = (part(6) + side_a[6]) * jnp.where(flags == 0, weight, 0.0)
        if guard:
            r2 = jnp.maximum(r2, 1e-2)
            l2 = jnp.maximum(l2, 1e-2)
        r_inv = lax.rsqrt(r2)
        l_inv = lax.rsqrt(l2)
        cl = c * l_inv
        k2 = c * r_inv - cl
        along = cl * (l_inv * l_inv) * (y[0] * dv[0] + y[1] * dv[1] + y[2] * dv[2])
        return [acc[i] + (k2 * dv[i] + along * y[i]) for i in range(3)]

    def pair(q, carry):
        tile = pairs[0, q]
        partner = pairs[1, q]
        sx = pairs[2, q]
        sy = pairs[3, q]
        own = full[tile]
        dx = (sx * 8).astype(F32)
        dy = (sy * (points // 16)).astype(F32)
        side_a = []
        for c in range(11):
            row = own[c : c + 1]
            if c in (0, 3):
                row = row - dx
            if c in (1, 4):
                row = row - dy
            side_a.append(jnp.broadcast_to(row, (8, points)))

        def finish(acc):
            for i in range(3):
                total[tile, i] += acc[i]

        zero = [jnp.zeros((8, points), F32)] * 3

        @pl.when((sx == 0) & (sy == 0))
        def _():
            acc = zero
            low, high = words[q, 0:8], words[q, 8:16]
            for x in range(8):
                for z, word in ((0, low), (1, high)):
                    block = turned[partner, pl.ds(x + 64 * z, 8, stride=8), :]
                    acc = bonds(block, side_a, word & (1 << x), acc, True)
            finish(acc)

        @pl.when((sx != 0) & (sy == 0))
        def _():
            acc = zero
            low, high = words[q, 0:8], words[q, 8:16]
            x0 = jnp.where(sx > 0, 0, 5)
            for k in range(3):
                for z, word in ((0, low), (1, high)):
                    block = turned[partner, pl.ds(x0 + k + 64 * z, 8, stride=8), :]
                    acc = bonds(block, side_a, word & (1 << (x0 + k)), acc, False)
            finish(acc)

        @pl.when((sx == 0) & (sy != 0))
        def _():
            acc = zero
            y0 = jnp.where(sy > 0, 0, 5)
            bit = jnp.left_shift(1, lax.broadcasted_iota(jnp.int32, (8, points), 0))
            for k in range(3):
                for z in range(2):
                    start = (y0 + k) * 8 + 64 * z
                    block = turned[partner, pl.ds(pl.multiple_of(start, 8), 8), :]
                    word = jnp.broadcast_to(words[q, pl.ds(y0 + k + 8 * z, 1), :], (8, points))
                    acc = bonds(block, side_a, word & bit, acc, False)
            finish(acc)

        @pl.when((sx != 0) & (sy != 0))
        def _():
            acc = zero
            x0 = jnp.where(sx > 0, 0, 5)
            y0 = jnp.where(sy > 0, 0, 4)
            word = jnp.concatenate([words[q, pl.ds(y0, 4), :], words[q, pl.ds(y0 + 8, 4), :]], axis=0)
            for k in range(3):
                start = x0 + k + 8 * y0
                block = jnp.concatenate(
                    [
                        turned[partner, pl.ds(start, 4, stride=8), :],
                        turned[partner, pl.ds(start + 64, 4, stride=8), :],
                    ],
                    axis=0,
                )
                acc = bonds(block, side_a, word & (1 << (x0 + k)), acc, False)
            finish(acc)

        return carry

    lax.fori_loop(0, count[0], pair, 0)

    def close(j, carry):
        image[j] = jnp.sum(total[j], axis=1)
        return carry

    lax.fori_loop(0, rows, close, 0, unroll=4)
    if first:
        for out in sends:
            out[...] = jnp.zeros_like(out)

        def ghost_rows(i, carry):
            for c, out in zip(DIRS, sends):
                out[i, 0:3] = image[jnp.maximum(send[c, i], 0)]
            return carry

        lax.fori_loop(0, cap, ghost_rows, 0)


def to_side(block, ox, oy):
    n_x, n_y = lax.axis_size("gx"), lax.axis_size("gy")
    perm = []
    for x in range(n_x):
        for y in range(n_y):
            if 0 <= x + ox < n_x and 0 <= y + oy < n_y:
                perm.append((x * n_y + y, (x + ox) * n_y + y + oy))
    return lax.ppermute(block, ("gx", "gy"), perm)


def share(sends):
    by_dir = dict(zip(DIRS, sends))
    return [to_side(by_dir[8 - e], (8 - e) // 3 - 1, (8 - e) % 3 - 1) for e in DIRS]


def on_device(jitter, displacement, modulus, start_vec, old_home, ghost_send, pair_list, pair_count, broken):
    tiles = old_home.shape[0]
    points = jitter.shape[2]
    cap = ghost_send.shape[2]
    width_y = lax.axis_size("gy")
    anchor = old_home // tiles
    old_slot = old_home % tiles
    off_x = anchor // width_y - lax.axis_index("gx")
    off_y = anchor % width_y - lax.axis_index("gy")
    side = jnp.where(off_x == -1, 0, jnp.where(off_x == 1, 1, jnp.where(off_y == -1, 2, jnp.where(off_y == 1, 3, 4))))
    index = jnp.arange(tiles, dtype=jnp.int32)
    earlier = (side[:, None] == side[None, :]) & (index[:, None] < index[None, :])
    ranked = jnp.sum(earlier.astype(jnp.int32), axis=0)
    cell = jnp.where(side < 4, side * CAP + ranked, -1)
    hit = cell[:, None] == jnp.arange(4 * CAP, dtype=jnp.int32)[None, :]
    wanted = jnp.sum(jnp.where(hit, old_slot[:, None], 0), axis=0).reshape(4, CAP)
    moves = ((-1, 0), (1, 0), (0, -1), (0, 1))
    twin = (1, 0, 3, 2)
    asked = jnp.stack([to_side(wanted[twin[d]], *moves[twin[d]]) for d in range(4)])
    pick = jnp.where(side < 4, tiles + cell, old_slot)

    state = (jitter, displacement, modulus, start_vec)
    handed = pl.pallas_call(
        hand_kernel,
        out_shape=[jax.ShapeDtypeStruct((CAP, 16, points), F32)] * 4,
        in_specs=[SMEM] + [VMEM] * 4,
        out_specs=[VMEM] * 4,
        compiler_params=LIMIT,
    )(asked, *state)
    arrived = [to_side(handed[twin[d]], *moves[twin[d]]) for d in range(4)]
    lat = lattice(points)
    lat8 = jnp.concatenate([lat, jnp.zeros((5, points), F32)], axis=0)
    ghost_shape = jax.ShapeDtypeStruct((cap, 16, points), F32)
    local, *sends = pl.pallas_call(
        settle_kernel,
        out_shape=[jax.ShapeDtypeStruct((tiles, 16, points), F32)] + [ghost_shape] * 8,
        in_specs=[SMEM] * 2 + [VMEM] * 9,
        out_specs=[VMEM] * 9,
        scratch_shapes=[pltpu.VMEM((tiles + 4 * CAP, 16, points), F32)],
        compiler_params=LIMIT,
    )(pick, ghost_send[0], lat8, *state, *arrived)
    ghosts = share(sends)
    rows = tiles + 9 * cap
    scratch = [
        pltpu.VMEM((rows, 16, points), F32),
        pltpu.VMEM((rows, points, 16), F32),
        pltpu.VMEM((tiles, 3, 8, points), F32),
    ]
    image_shape = jax.ShapeDtypeStruct((tiles, 3, points), F32)
    head = (pair_list[0], pair_count, ghost_send[0], broken, local, *ghosts)
    first_image, *image_sends = pl.pallas_call(
        functools.partial(apply_kernel, True),
        out_shape=[image_shape] + [jax.ShapeDtypeStruct((cap, 8, points), F32)] * 8,
        in_specs=[SMEM] * 3 + [VMEM] * 10,
        out_specs=[VMEM] * 9,
        scratch_shapes=scratch,
        compiler_params=LIMIT,
    )(*head)
    image_ghosts = share(image_sends)
    second_image = pl.pallas_call(
        functools.partial(apply_kernel, False),
        out_shape=image_shape,
        in_specs=[SMEM] * 3 + [VMEM] * 19,
        out_specs=VMEM,
        scratch_shapes=scratch,
        compiler_params=LIMIT,
    )(*head, first_image, *image_ghosts)
    return (first_image, second_image)


def solution(mesh):
    split = ("gx", "gy")
    spec3, spec2, spec1 = P(split, None, None), P(split, None), P(split)
    return jax.shard_map(
        on_device,
        mesh=mesh,
        in_specs=(spec3, spec3, spec2, spec3, spec1, spec3, spec3, spec1, spec3),
        out_specs=(spec3, spec3),
        check_vma=False,
    )
```

```python
import functools
import jax
import jax.numpy as jnp
from jax import lax
from jax.experimental import pallas as pl
from jax.experimental.pallas import tpu as pltpu
from jax.sharding import PartitionSpec as P

CAP = 16
F32 = jnp.float32
VMEM = pl.BlockSpec(memory_space=pltpu.VMEM)
SMEM = pl.BlockSpec(memory_space=pltpu.SMEM)
LIMIT = pltpu.CompilerParams(vmem_limit_bytes=48 * 1024 * 1024)
DIRS = (0, 1, 2, 3, 5, 6, 7, 8)


def lattice(points):
    counter = jnp.arange(points, dtype=jnp.int32)
    return jnp.stack([counter % 8, counter // 8 % (points // 16), counter // (points // 2)]).astype(F32)


def hand_kernel(asked, jit, disp, mod, vec, *outs):
    for out in outs:
        out[...] = jnp.zeros_like(out)

    def body(i, carry):
        for d, out in enumerate(outs):
            row = asked[d, i]
            out[i, 0:3] = jit[row]
            out[i, 3:6] = disp[row]
            out[i, 6:7] = mod[pl.ds(row, 1)]
            out[i, 8:11] = vec[row]
        return carry

    lax.fori_loop(0, CAP, body, 0)


def settle_kernel(pick, send, lat8, jit, disp, mod, vec, in0, in1, in2, in3, local, *rest):
    outs, pool = rest[:8], rest[8]
    rows = jit.shape[0]
    pool[0:rows] = jnp.zeros((rows,) + pool.shape[1:], F32)
    pool[0:rows, 0:3, :] = jit[...]
    pool[0:rows, 3:6, :] = disp[...]
    pool[0:rows, 8:11, :] = vec[...]

    def put_mod(j, carry):
        pool[j, 6:7, :] = mod[pl.ds(j, 1)]
        return carry

    lax.fori_loop(0, rows, put_mod, 0, unroll=8)
    for d, arrived in enumerate((in0, in1, in2, in3)):
        pool[rows + d * CAP : rows + (d + 1) * CAP] = arrived[...]
    points = jit.shape[2]
    sub = lax.broadcasted_iota(jnp.int32, (8, points), 0)
    scale = jnp.where(sub == 6, 0.05, 1.0)
    moved = (sub >= 3) & (sub < 6)

    def settle(j, carry):
        held = pool[pick[j]]
        low = held[0:8]
        base = low + lat8[...]
        shifted = jnp.where(moved, pltpu.roll(base, 3, 0), 0.0)
        local[j, 0:8] = low * scale + jnp.where(moved, 0.0, lat8[...]) + shifted
        local[j, 8:16] = held[8:16]
        return carry

    lax.fori_loop(0, rows, settle, 0, unroll=8)

    def ghosts(i, carry):
        for c, out in zip(DIRS, outs):
            out[i] = local[jnp.maximum(send[c, i], 0)]
        return carry

    lax.fori_loop(0, outs[0].shape[0], ghosts, 0)


def apply_kernel(first, pairs, order, bounds, send, words, local, *rest):
    ghosts, rest = rest[:8], rest[8:]
    if not first:
        field, field_ghosts, rest = rest[0], rest[1:9], rest[9:]
    image, rest = rest[0], rest[1:]
    if first:
        sends, rest = rest[:8], rest[8:]
    full, turned, total = rest
    rows, _, points = local.shape
    cap = ghosts[0].shape[0]
    full[0:rows] = local[...]
    full[rows + 4 * cap : rows + 5 * cap] = jnp.zeros((cap,) + full.shape[1:], F32)
    for e, ghost in zip(DIRS, ghosts):
        full[rows + e * cap : rows + (e + 1) * cap] = ghost[...]
    if not first:
        full[0:rows, 8:11, :] = field[...]
        for e, ghost in zip(DIRS, field_ghosts):
            full[rows + e * cap : rows + (e + 1) * cap, 8:16, :] = ghost[...]

    def turn(j, carry):
        turned[j] = jnp.transpose(full[j])
        return carry

    lax.fori_loop(0, full.shape[0], turn, 0, unroll=8)
    total[...] = jnp.zeros_like(total)

    def bonds(side_b, side_a, flags, acc, guard):
        part = lambda c: side_b[:, c : c + 1]
        xi = [part(c) - side_a[c] for c in range(3)]
        y = [part(3 + c) - side_a[3 + c] for c in range(3)]
        dv = [part(8 + c) - side_a[8 + c] for c in range(3)]
        r2 = xi[0] * xi[0] + xi[1] * xi[1] + xi[2] * xi[2]
        l2 = y[0] * y[0] + y[1] * y[1] + y[2] * y[2]
        weight = jnp.maximum(1.0 - r2 * (1.0 / 9.0), 0.0)
        c = (part(6) + side_a[6]) * jnp.where(flags == 0, weight, 0.0)
        if guard:
            r2 = jnp.maximum(r2, 1e-2)
            l2 = jnp.maximum(l2, 1e-2)
        r_inv = lax.rsqrt(r2)
        l_inv = lax.rsqrt(l2)
        cl = c * l_inv
        k2 = c * r_inv - cl
        along = cl * (l_inv * l_inv) * (y[0] * dv[0] + y[1] * dv[1] + y[2] * dv[2])
        return [acc[i] + (k2 * dv[i] + along * y[i]) for i in range(3)]

    def pair(kind, slot):
        live = slot >= 0
        q = jnp.maximum(slot, 0)
        tile = pairs[0, q]
        partner = pairs[1, q]
        sx = pairs[2, q]
        sy = pairs[3, q]
        dx = (sx * 8).astype(F32)
        dy = (sy * (points // 16)).astype(F32)
        side_a = []
        for c in range(11):
            if c == 7:
                side_a.append(None)
                continue
            row = full[tile, c : c + 1]
            if c in (0, 3) and kind & 1:
                row = row - dx
            if c in (1, 4) and kind & 2:
                row = row - dy
            side_a.append(jnp.broadcast_to(row, (8, points)))
        acc = [jnp.zeros((8, points), F32)] * 3
        x0 = jnp.where(sx > 0, 0, 5) if kind & 1 else 0
        if kind < 2:
            for k in range(3 if kind else 8):
                for z in range(2):
                    block = turned[partner, pl.ds(x0 + k + 64 * z, 8, stride=8), :]
                    flags = words[q, 8 * z : 8 * z + 8] & jnp.left_shift(1, x0 + k)
                    acc = bonds(block, side_a, flags, acc, kind == 0)
        elif kind == 2:
            y0 = jnp.where(sy > 0, 0, 5)
            bit = jnp.left_shift(1, lax.broadcasted_iota(jnp.int32, (8, points), 0))
            for k in range(3):
                for z in range(2):
                    start = (y0 + k) * 8 + 64 * z
                    block = turned[partner, pl.ds(pl.multiple_of(start, 8), 8), :]
                    word = jnp.broadcast_to(words[q, pl.ds(y0 + k + 8 * z, 1), :], (8, points))
                    acc = bonds(block, side_a, word & bit, acc, False)
        else:
            y0 = jnp.where(sy > 0, 0, 4)
            word = jnp.concatenate([words[q, pl.ds(y0, 4), :], words[q, pl.ds(y0 + 8, 4), :]], axis=0)
            for k in range(3):
                start = x0 + k + 8 * y0
                block = jnp.concatenate(
                    [
                        turned[partner, pl.ds(start, 4, stride=8), :],
                        turned[partner, pl.ds(start + 64, 4, stride=8), :],
                    ],
                    axis=0,
                )
                acc = bonds(block, side_a, word & jnp.left_shift(1, x0 + k), acc, False)
        return tile, [jnp.where(live, term, 0.0) for term in acc]

    for kind, width in enumerate(UNROLL):

        def step(i, carry, kind=kind, width=width):
            done = [pair(kind, order[i * width + u]) for u in range(width)]
            for tile, acc in done:
                for c in range(3):
                    total[tile, c] += acc[c]
            return carry

        lax.fori_loop(bounds[2 * kind], bounds[2 * kind + 1], step, 0)

    def close(j, carry):
        image[j] = jnp.sum(total[j], axis=1)
        return carry

    lax.fori_loop(0, rows, close, 0, unroll=4)
    if first:
        for out in sends:
            out[...] = jnp.zeros_like(out)

        def ghost_rows(i, carry):
            for c, out in zip(DIRS, sends):
                out[i, 0:3] = image[jnp.maximum(send[c, i], 0)]
            return carry

        lax.fori_loop(0, cap, ghost_rows, 0)


def exchange_kernel(offsets, *refs):
    n = len(offsets)
    ins, outs, send_sem, recv_sem = refs[:n], refs[n : 2 * n], refs[2 * n], refs[2 * n + 1]
    n_x, n_y = lax.axis_size("gx"), lax.axis_size("gy")
    x, y = lax.axis_index("gx"), lax.axis_index("gy")

    def exists(ox, oy):
        return (x + ox >= 0) & (x + ox < n_x) & (y + oy >= 0) & (y + oy < n_y)

    barrier = pltpu.get_barrier_semaphore()
    for ox, oy in offsets:

        @pl.when(exists(ox, oy))
        def _():
            pl.semaphore_signal(
                barrier, inc=1, device_id=(x + ox, y + oy), device_id_type=pl.DeviceIdType.MESH
            )

    peers = sum(jnp.where(exists(ox, oy), 1, 0) for ox, oy in offsets)
    pl.semaphore_wait(barrier, peers)

    def copy(d):
        ox, oy = offsets[d]
        back = offsets.index((-ox, -oy))
        return pltpu.make_async_remote_copy(
            src_ref=ins[d],
            dst_ref=outs[back],
            send_sem=send_sem.at[d],
            recv_sem=recv_sem.at[back],
            device_id=(x + ox, y + oy),
            device_id_type=pl.DeviceIdType.MESH,
        )

    for d, (ox, oy) in enumerate(offsets):

        @pl.when(exists(ox, oy))
        def _():
            copy(d).start()

        @pl.when(jnp.logical_not(exists(ox, oy)))
        def _():
            outs[d][...] = jnp.zeros_like(outs[d])

    for d, (ox, oy) in enumerate(offsets):

        @pl.when(exists(ox, oy))
        def _():
            copy(d).wait_send()
            copy(offsets.index((-ox, -oy))).wait_recv()


def exchange(blocks, offsets, ident):
    n = len(offsets)
    return pl.pallas_call(
        functools.partial(exchange_kernel, offsets),
        out_shape=[jax.ShapeDtypeStruct(b.shape, b.dtype) for b in blocks],
        in_specs=[VMEM] * n,
        out_specs=[VMEM] * n,
        scratch_shapes=[pltpu.SemaphoreType.DMA((n,)), pltpu.SemaphoreType.DMA((n,))],
        compiler_params=pltpu.CompilerParams(
            collective_id=ident, has_side_effects=True, vmem_limit_bytes=16 * 1024 * 1024
        ),
    )(*blocks)


SIDES = ((-1, 0), (1, 0), (0, -1), (0, 1))
AROUND = tuple((e // 3 - 1, e % 3 - 1) for e in DIRS)
UNROLL = (1, 4, 4, 8)


def by_kind(pair_list, count):
    pairs = pair_list.shape[1]
    slot = jnp.arange(pairs, dtype=jnp.int32)
    kind = (pair_list[2] != 0).astype(jnp.int32) + 2 * (pair_list[3] != 0).astype(jnp.int32)
    kind = jnp.where(slot < count, kind, 4)
    earlier = (kind[:, None] == kind[None, :]) & (slot[:, None] < slot[None, :])
    place = jnp.sum(earlier.astype(jnp.int32), axis=0)
    start, bounds = jnp.int32(0), []
    for k, width in enumerate(UNROLL):
        members = jnp.sum((kind == k).astype(jnp.int32))
        place = place + jnp.where(kind == k, start, 0)
        bounds += [start // width, (start + members + width - 1) // width]
        start = start + (members + 7) // 8 * 8
    place = jnp.where(kind < 4, place, -1)
    hit = place[:, None] == jnp.arange(pairs + 32, dtype=jnp.int32)[None, :]
    order = jnp.sum(jnp.where(hit, slot[:, None] + 1, 0), axis=0) - 1
    return order, jnp.stack(bounds)


def on_device(jitter, displacement, modulus, start_vec, old_home, ghost_send, pair_list, pair_count, broken):
    tiles = old_home.shape[0]
    points = jitter.shape[2]
    cap = ghost_send.shape[2]
    width_y = lax.axis_size("gy")
    anchor = old_home // tiles
    old_slot = old_home % tiles
    off_x = anchor // width_y - lax.axis_index("gx")
    off_y = anchor % width_y - lax.axis_index("gy")
    side = jnp.where(off_x == -1, 0, jnp.where(off_x == 1, 1, jnp.where(off_y == -1, 2, jnp.where(off_y == 1, 3, 4))))
    index = jnp.arange(tiles, dtype=jnp.int32)
    earlier = (side[:, None] == side[None, :]) & (index[:, None] < index[None, :])
    ranked = jnp.sum(earlier.astype(jnp.int32), axis=0)
    cell = jnp.where(side < 4, side * CAP + ranked, -1)
    hit = cell[:, None] == jnp.arange(4 * CAP, dtype=jnp.int32)[None, :]
    wanted = jnp.sum(jnp.where(hit, old_slot[:, None], 0), axis=0).reshape(4, CAP)
    requests = [jnp.pad(wanted[d : d + 1], ((0, 7), (0, 128 - CAP))) for d in range(4)]
    asked = jnp.concatenate([r[0:1] for r in exchange(requests, SIDES, 0)], axis=0)
    pick = jnp.where(side < 4, tiles + cell, old_slot)

    state = (jitter, displacement, modulus, start_vec)
    handed = pl.pallas_call(
        hand_kernel,
        out_shape=[jax.ShapeDtypeStruct((CAP, 16, points), F32)] * 4,
        in_specs=[SMEM] + [VMEM] * 4,
        out_specs=[VMEM] * 4,
        compiler_params=LIMIT,
    )(asked, *state)
    arrived = exchange(handed, SIDES, 1)
    lat = lattice(points)
    lat8 = jnp.concatenate([lat, jnp.zeros((5, points), F32)], axis=0)
    ghost_shape = jax.ShapeDtypeStruct((cap, 16, points), F32)
    local, *sends = pl.pallas_call(
        settle_kernel,
        out_shape=[jax.ShapeDtypeStruct((tiles, 16, points), F32)] + [ghost_shape] * 8,
        in_specs=[SMEM] * 2 + [VMEM] * 9,
        out_specs=[VMEM] * 9,
        scratch_shapes=[pltpu.VMEM((tiles + 4 * CAP, 16, points), F32)],
        compiler_params=LIMIT,
    )(pick, ghost_send[0], lat8, *state, *arrived)
    ghosts = exchange(sends, AROUND, 2)
    rows = tiles + 9 * cap
    scratch = [
        pltpu.VMEM((rows, 16, points), F32),
        pltpu.VMEM((rows, points, 16), F32),
        pltpu.VMEM((tiles, 3, 8, points), F32),
    ]
    image_shape = jax.ShapeDtypeStruct((tiles, 3, points), F32)
    order, bounds = by_kind(pair_list[0], pair_count[0])
    head = (pair_list[0], order, bounds, ghost_send[0], broken, local, *ghosts)
    first_image, *image_sends = pl.pallas_call(
        functools.partial(apply_kernel, True),
        out_shape=[image_shape] + [jax.ShapeDtypeStruct((cap, 8, points), F32)] * 8,
        in_specs=[SMEM] * 4 + [VMEM] * 10,
        out_specs=[VMEM] * 9,
        scratch_shapes=scratch,
        compiler_params=LIMIT,
    )(*head)
    image_ghosts = exchange(image_sends, AROUND, 3)
    second_image = pl.pallas_call(
        functools.partial(apply_kernel, False),
        out_shape=image_shape,
        in_specs=[SMEM] * 4 + [VMEM] * 19,
        out_specs=VMEM,
        scratch_shapes=scratch,
        compiler_params=LIMIT,
    )(*head, first_image, *image_ghosts)
    return (first_image, second_image)


def solution(mesh):
    split = ("gx", "gy")
    spec3, spec2, spec1 = P(split, None, None), P(split, None), P(split)
    return jax.shard_map(
        on_device,
        mesh=mesh,
        in_specs=(spec3, spec3, spec2, spec3, spec1, spec3, spec3, spec1, spec3),
        out_specs=(spec3, spec3),
        check_vma=False,
    )
```

```python
import functools
import jax
import jax.numpy as jnp
from jax import lax
from jax.experimental import pallas as pl
from jax.experimental.pallas import tpu as pltpu
from jax.sharding import PartitionSpec as P

CAP = 16
F32 = jnp.float32
VMEM = pl.BlockSpec(memory_space=pltpu.VMEM)
SMEM = pl.BlockSpec(memory_space=pltpu.SMEM)
LIMIT = pltpu.CompilerParams(vmem_limit_bytes=48 * 1024 * 1024)
DIRS = (0, 1, 2, 3, 5, 6, 7, 8)
FIELDS = (0, 1, 2, 3, 4, 5, 6, 8, 9, 10)


def lattice(points):
    counter = jnp.arange(points, dtype=jnp.int32)
    return jnp.stack([counter % 8, counter // 8 % (points // 16), counter // (points // 2)]).astype(F32)


def hand_kernel(asked, jit, disp, mod, vec, *outs):
    for out in outs:
        out[...] = jnp.zeros_like(out)

    def body(i, carry):
        for d, out in enumerate(outs):
            row = asked[d, i]
            out[i, 0:3] = jit[row]
            out[i, 3:6] = disp[row]
            out[i, 6:7] = mod[pl.ds(row, 1)]
            out[i, 8:11] = vec[row]
        return carry

    lax.fori_loop(0, CAP, body, 0)


def settle_kernel(pick, send, lat8, jit, disp, mod, vec, in0, in1, in2, in3, local, *rest):
    outs, pool = rest[:8], rest[8]
    rows = jit.shape[0]
    pool[0:rows] = jnp.zeros((rows,) + pool.shape[1:], F32)
    pool[0:rows, 0:3, :] = jit[...]
    pool[0:rows, 3:6, :] = disp[...]
    pool[0:rows, 8:11, :] = vec[...]

    def put_mod(j, carry):
        pool[j, 6:7, :] = mod[pl.ds(j, 1)]
        return carry

    lax.fori_loop(0, rows, put_mod, 0, unroll=8)
    for d, arrived in enumerate((in0, in1, in2, in3)):
        pool[rows + d * CAP : rows + (d + 1) * CAP] = arrived[...]
    points = jit.shape[2]
    sub = lax.broadcasted_iota(jnp.int32, (8, points), 0)
    scale = jnp.where(sub == 6, 0.05, 1.0)
    moved = (sub >= 3) & (sub < 6)

    def settle(j, carry):
        held = pool[pick[j]]
        low = held[0:8]
        base = low + lat8[...]
        shifted = jnp.where(moved, pltpu.roll(base, 3, 0), 0.0)
        local[j, 0:8] = low * scale + jnp.where(moved, 0.0, lat8[...]) + shifted
        local[j, 8:16] = held[8:16]
        return carry

    lax.fori_loop(0, rows, settle, 0, unroll=8)

    def ghosts(i, carry):
        for c, out in zip(DIRS, outs):
            out[i] = local[jnp.maximum(send[c, i], 0)]
        return carry

    lax.fori_loop(0, outs[0].shape[0], ghosts, 0)


def apply_kernel(first, pairs, order, bounds, send, spread, words, local, *rest):
    ghosts, rest = rest[:8], rest[8:]
    if not first:
        field, field_ghosts, rest = rest[0], rest[1:9], rest[9:]
    image, rest = rest[0], rest[1:]
    if first:
        sends, rest = rest[:8], rest[8:]
    full, turned, total = rest
    rows, _, points = local.shape
    cap = ghosts[0].shape[0]
    full[0:rows] = local[...]
    full[rows + 4 * cap : rows + 5 * cap] = jnp.zeros((cap,) + full.shape[1:], F32)
    for e, ghost in zip(DIRS, ghosts):
        full[rows + e * cap : rows + (e + 1) * cap] = ghost[...]
    if not first:
        full[0:rows, 8:11, :] = field[...]
        for e, ghost in zip(DIRS, field_ghosts):
            full[rows + e * cap : rows + (e + 1) * cap, 8:16, :] = ghost[...]

    def turn(j, carry):
        state = full[j]
        high = state.astype(jnp.bfloat16).astype(F32)
        rest_of = state - high
        middle = rest_of.astype(jnp.bfloat16).astype(F32)
        turned[j] = jnp.transpose(jnp.concatenate([high, middle, rest_of - middle], axis=0))
        return carry

    lax.fori_loop(0, full.shape[0], turn, 0, unroll=8)
    total[...] = jnp.zeros_like(total)

    def bonds(side_b, side_a, flags, acc, guard):
        part = lambda c: side_b[FIELDS.index(c)]
        xi = [part(c) - side_a[c] for c in range(3)]
        y = [part(3 + c) - side_a[3 + c] for c in range(3)]
        dv = [part(8 + c) - side_a[8 + c] for c in range(3)]
        r2 = xi[0] * xi[0] + xi[1] * xi[1] + xi[2] * xi[2]
        l2 = y[0] * y[0] + y[1] * y[1] + y[2] * y[2]
        weight = jnp.maximum(1.0 - r2 * (1.0 / 9.0), 0.0)
        c = (part(6) + side_a[6]) * jnp.where(flags == 0, weight, 0.0)
        if guard:
            c = jnp.where(r2 < 1e-2, 0.0, c)
            r2 = jnp.maximum(r2, 1e-2)
            l2 = jnp.maximum(l2, 1e-2)
        r_inv = lax.rsqrt(r2)
        l_inv = lax.rsqrt(l2)
        cl = c * l_inv
        k2 = c * r_inv - cl
        along = cl * (l_inv * l_inv) * (y[0] * dv[0] + y[1] * dv[1] + y[2] * dv[2])
        return [acc[i] + (k2 * dv[i] + along * y[i]) for i in range(3)]

    def pair(kind, slot):
        live = slot >= 0
        q = jnp.maximum(slot, 0)
        tile = pairs[0, q]
        partner = pairs[1, q]
        sx = pairs[2, q]
        sy = pairs[3, q]
        dx = (sx * 8).astype(F32)
        dy = (sy * (points // 16)).astype(F32)
        side_a = []
        for c in range(11):
            if c == 7:
                side_a.append(None)
                continue
            row = full[tile, c : c + 1]
            if c in (0, 3) and kind & 1:
                row = row - dx
            if c in (1, 4) and kind & 2:
                row = row - dy
            side_a.append(jnp.broadcast_to(row, (8, points)))
        blocks, words_of = [], []
        x0 = jnp.where(sx > 0, 0, 5) if kind & 1 else 0
        if kind < 2:
            for k in range(3 if kind else 8):
                for z in range(2):
                    block = turned[partner, pl.ds(x0 + k + 64 * z, 8, stride=8), :]
                    flags = words[q, 8 * z : 8 * z + 8] & jnp.left_shift(1, x0 + k)
                    blocks.append(block)
                    words_of.append(flags)
        elif kind == 2:
            y0 = jnp.where(sy > 0, 0, 5)
            bit = jnp.left_shift(1, lax.broadcasted_iota(jnp.int32, (8, points), 0))
            for k in range(3):
                for z in range(2):
                    start = (y0 + k) * 8 + 64 * z
                    block = turned[partner, pl.ds(pl.multiple_of(start, 8), 8), :]
                    word = jnp.broadcast_to(words[q, pl.ds(y0 + k + 8 * z, 1), :], (8, points))
                    blocks.append(block)
                    words_of.append(word & bit)
        else:
            y0 = jnp.where(sy > 0, 0, 4)
            word = jnp.concatenate([words[q, pl.ds(y0, 4), :], words[q, pl.ds(y0 + 8, 4), :]], axis=0)
            for k in range(3):
                start = x0 + k + 8 * y0
                block = jnp.concatenate(
                    [
                        turned[partner, pl.ds(start, 4, stride=8), :],
                        turned[partner, pl.ds(start + 64, 4, stride=8), :],
                    ],
                    axis=0,
                )
                blocks.append(block)
                words_of.append(word & jnp.left_shift(1, x0 + k))
        return live, tile, side_a, blocks, words_of

    for kind, width in enumerate(UNROLL):

        def step(i, carry, kind=kind, width=width):
            batch = [pair(kind, order[i * width + u]) for u in range(width)]
            stacked = jnp.concatenate([b for one in batch for b in one[3]], axis=0)
            wide = jnp.dot(stacked.astype(jnp.bfloat16), spread[...], preferred_element_type=F32)
            at = 0
            done = []
            for live, tile, side_a, blocks, words_of in batch:
                acc = [jnp.zeros((8, points), F32)] * 3
                for flags in words_of:
                    side_b = [wide[at : at + 8, n * points : (n + 1) * points] for n in range(len(FIELDS))]
                    acc = bonds(side_b, side_a, flags, acc, kind == 0)
                    at += 8
                done.append((tile, [jnp.where(live, term, 0.0) for term in acc]))
            for tile, acc in done:
                for c in range(3):
                    total[tile, c] += acc[c]
            return carry

        lax.fori_loop(bounds[2 * kind], bounds[2 * kind + 1], step, 0)

    def close(j, carry):
        image[j] = jnp.sum(total[j], axis=1)
        return carry

    lax.fori_loop(0, rows, close, 0, unroll=4)
    if first:
        for out in sends:
            out[...] = jnp.zeros_like(out)

        def ghost_rows(i, carry):
            for c, out in zip(DIRS, sends):
                out[i, 0:3] = image[jnp.maximum(send[c, i], 0)]
            return carry

        lax.fori_loop(0, cap, ghost_rows, 0)


def exchange_kernel(offsets, *refs):
    n = len(offsets)
    ins, outs, send_sem, recv_sem = refs[:n], refs[n : 2 * n], refs[2 * n], refs[2 * n + 1]
    n_x, n_y = lax.axis_size("gx"), lax.axis_size("gy")
    x, y = lax.axis_index("gx"), lax.axis_index("gy")

    def exists(ox, oy):
        return (x + ox >= 0) & (x + ox < n_x) & (y + oy >= 0) & (y + oy < n_y)

    barrier = pltpu.get_barrier_semaphore()
    for ox, oy in offsets:

        @pl.when(exists(ox, oy))
        def _():
            pl.semaphore_signal(
                barrier, inc=1, device_id=(x + ox, y + oy), device_id_type=pl.DeviceIdType.MESH
            )

    peers = sum(jnp.where(exists(ox, oy), 1, 0) for ox, oy in offsets)
    pl.semaphore_wait(barrier, peers)

    def copy(d):
        ox, oy = offsets[d]
        back = offsets.index((-ox, -oy))
        return pltpu.make_async_remote_copy(
            src_ref=ins[d],
            dst_ref=outs[back],
            send_sem=send_sem.at[d],
            recv_sem=recv_sem.at[back],
            device_id=(x + ox, y + oy),
            device_id_type=pl.DeviceIdType.MESH,
        )

    for d, (ox, oy) in enumerate(offsets):

        @pl.when(exists(ox, oy))
        def _():
            copy(d).start()

        @pl.when(jnp.logical_not(exists(ox, oy)))
        def _():
            outs[d][...] = jnp.zeros_like(outs[d])

    for d, (ox, oy) in enumerate(offsets):

        @pl.when(exists(ox, oy))
        def _():
            copy(d).wait_send()
            copy(offsets.index((-ox, -oy))).wait_recv()


def exchange(blocks, offsets, ident):
    n = len(offsets)
    return pl.pallas_call(
        functools.partial(exchange_kernel, offsets),
        out_shape=[jax.ShapeDtypeStruct(b.shape, b.dtype) for b in blocks],
        in_specs=[VMEM] * n,
        out_specs=[VMEM] * n,
        scratch_shapes=[pltpu.SemaphoreType.DMA((n,)), pltpu.SemaphoreType.DMA((n,))],
        compiler_params=pltpu.CompilerParams(
            collective_id=ident, has_side_effects=True, vmem_limit_bytes=16 * 1024 * 1024
        ),
    )(*blocks)


SIDES = ((-1, 0), (1, 0), (0, -1), (0, 1))
AROUND = tuple((e // 3 - 1, e % 3 - 1) for e in DIRS)
UNROLL = (1, 4, 4, 8)


def by_kind(pair_list, count):
    pairs = pair_list.shape[1]
    slot = jnp.arange(pairs, dtype=jnp.int32)
    kind = (pair_list[2] != 0).astype(jnp.int32) + 2 * (pair_list[3] != 0).astype(jnp.int32)
    kind = jnp.where(slot < count, kind, 4)
    earlier = (kind[:, None] == kind[None, :]) & (slot[:, None] < slot[None, :])
    place = jnp.sum(earlier.astype(jnp.int32), axis=0)
    start, bounds = jnp.int32(0), []
    for k, width in enumerate(UNROLL):
        members = jnp.sum((kind == k).astype(jnp.int32))
        place = place + jnp.where(kind == k, start, 0)
        bounds += [start // width, (start + members + width - 1) // width]
        start = start + (members + 7) // 8 * 8
    place = jnp.where(kind < 4, place, -1)
    hit = place[:, None] == jnp.arange(pairs + 32, dtype=jnp.int32)[None, :]
    order = jnp.sum(jnp.where(hit, slot[:, None] + 1, 0), axis=0) - 1
    return order, jnp.stack(bounds)


def on_device(jitter, displacement, modulus, start_vec, old_home, ghost_send, pair_list, pair_count, broken):
    tiles = old_home.shape[0]
    points = jitter.shape[2]
    cap = ghost_send.shape[2]
    width_y = lax.axis_size("gy")
    anchor = old_home // tiles
    old_slot = old_home % tiles
    off_x = anchor // width_y - lax.axis_index("gx")
    off_y = anchor % width_y - lax.axis_index("gy")
    side = jnp.where(off_x == -1, 0, jnp.where(off_x == 1, 1, jnp.where(off_y == -1, 2, jnp.where(off_y == 1, 3, 4))))
    index = jnp.arange(tiles, dtype=jnp.int32)
    earlier = (side[:, None] == side[None, :]) & (index[:, None] < index[None, :])
    ranked = jnp.sum(earlier.astype(jnp.int32), axis=0)
    cell = jnp.where(side < 4, side * CAP + ranked, -1)
    hit = cell[:, None] == jnp.arange(4 * CAP, dtype=jnp.int32)[None, :]
    wanted = jnp.sum(jnp.where(hit, old_slot[:, None], 0), axis=0).reshape(4, CAP)
    requests = [jnp.pad(wanted[d : d + 1], ((0, 7), (0, 128 - CAP))) for d in range(4)]
    asked = jnp.concatenate([r[0:1] for r in exchange(requests, SIDES, 0)], axis=0)
    pick = jnp.where(side < 4, tiles + cell, old_slot)

    state = (jitter, displacement, modulus, start_vec)
    handed = pl.pallas_call(
        hand_kernel,
        out_shape=[jax.ShapeDtypeStruct((CAP, 16, points), F32)] * 4,
        in_specs=[SMEM] + [VMEM] * 4,
        out_specs=[VMEM] * 4,
        compiler_params=LIMIT,
    )(asked, *state)
    arrived = exchange(handed, SIDES, 1)
    lat = lattice(points)
    lat8 = jnp.concatenate([lat, jnp.zeros((5, points), F32)], axis=0)
    ghost_shape = jax.ShapeDtypeStruct((cap, 16, points), F32)
    local, *sends = pl.pallas_call(
        settle_kernel,
        out_shape=[jax.ShapeDtypeStruct((tiles, 16, points), F32)] + [ghost_shape] * 8,
        in_specs=[SMEM] * 2 + [VMEM] * 9,
        out_specs=[VMEM] * 9,
        scratch_shapes=[pltpu.VMEM((tiles + 4 * CAP, 16, points), F32)],
        compiler_params=LIMIT,
    )(pick, ghost_send[0], lat8, *state, *arrived)
    ghosts = exchange(sends, AROUND, 2)
    rows = tiles + 9 * cap
    scratch = [
        pltpu.VMEM((rows, 16, points), F32),
        pltpu.VMEM((rows, points, 48), F32),
        pltpu.VMEM((tiles, 3, 8, points), F32),
    ]
    image_shape = jax.ShapeDtypeStruct((tiles, 3, points), F32)
    order, bounds = by_kind(pair_list[0], pair_count[0])
    row = jnp.arange(48, dtype=jnp.int32)[:, None] % 16
    field = jnp.repeat(jnp.array(FIELDS, jnp.int32), points)[None, :]
    spread = (row == field).astype(jnp.bfloat16)
    head = (pair_list[0], order, bounds, ghost_send[0], spread, broken, local, *ghosts)
    first_image, *image_sends = pl.pallas_call(
        functools.partial(apply_kernel, True),
        out_shape=[image_shape] + [jax.ShapeDtypeStruct((cap, 8, points), F32)] * 8,
        in_specs=[SMEM] * 4 + [VMEM] * 11,
        out_specs=[VMEM] * 9,
        scratch_shapes=scratch,
        compiler_params=LIMIT,
    )(*head)
    image_ghosts = exchange(image_sends, AROUND, 3)
    second_image = pl.pallas_call(
        functools.partial(apply_kernel, False),
        out_shape=image_shape,
        in_specs=[SMEM] * 4 + [VMEM] * 20,
        out_specs=VMEM,
        scratch_shapes=scratch,
        compiler_params=LIMIT,
    )(*head, first_image, *image_ghosts)
    return (first_image, second_image)


def solution(mesh):
    split = ("gx", "gy")
    spec3, spec2, spec1 = P(split, None, None), P(split, None), P(split)
    return jax.shard_map(
        on_device,
        mesh=mesh,
        in_specs=(spec3, spec3, spec2, spec3, spec1, spec3, spec3, spec1, spec3),
        out_specs=(spec3, spec3),
        check_vma=False,
    )
```

```python
import functools
import jax
import jax.numpy as jnp
from jax import lax
from jax.experimental import pallas as pl
from jax.experimental.pallas import tpu as pltpu
from jax.sharding import PartitionSpec as P

CAP = 16
F32 = jnp.float32
VMEM = pl.BlockSpec(memory_space=pltpu.VMEM)
SMEM = pl.BlockSpec(memory_space=pltpu.SMEM)
LIMIT = pltpu.CompilerParams(vmem_limit_bytes=48 * 1024 * 1024)
DIRS = (0, 1, 2, 3, 5, 6, 7, 8)
FIELDS = (0, 1, 2, 3, 4, 5, 6, 8, 9, 10)


def lattice(points):
    counter = jnp.arange(points, dtype=jnp.int32)
    return jnp.stack([counter % 8, counter // 8 % (points // 16), counter // (points // 2)]).astype(F32)


def hand_kernel(asked, jit, disp, mod, vec, *outs):
    for out in outs:
        out[...] = jnp.zeros_like(out)

    def body(i, carry):
        for d, out in enumerate(outs):
            row = asked[d, i]
            out[i, 0:3] = jit[row]
            out[i, 3:6] = disp[row]
            out[i, 6:7] = mod[pl.ds(row, 1)]
            out[i, 8:11] = vec[row]
        return carry

    lax.fori_loop(0, CAP, body, 0)


def settle_kernel(pick, send, lat8, jit, disp, mod, vec, in0, in1, in2, in3, local, *rest):
    outs, pool = rest[:8], rest[8]
    rows = jit.shape[0]
    pool[0:rows] = jnp.zeros((rows,) + pool.shape[1:], F32)
    pool[0:rows, 0:3, :] = jit[...]
    pool[0:rows, 3:6, :] = disp[...]
    pool[0:rows, 8:11, :] = vec[...]

    def put_mod(j, carry):
        pool[j, 6:7, :] = mod[pl.ds(j, 1)]
        return carry

    lax.fori_loop(0, rows, put_mod, 0, unroll=8)
    for d, arrived in enumerate((in0, in1, in2, in3)):
        pool[rows + d * CAP : rows + (d + 1) * CAP] = arrived[...]
    points = jit.shape[2]
    sub = lax.broadcasted_iota(jnp.int32, (8, points), 0)
    scale = jnp.where(sub == 6, 0.05, 1.0)
    moved = (sub >= 3) & (sub < 6)

    def settle(j, carry):
        held = pool[pick[j]]
        low = held[0:8]
        base = low + lat8[...]
        shifted = jnp.where(moved, pltpu.roll(base, 3, 0), 0.0)
        local[j, 0:8] = low * scale + jnp.where(moved, 0.0, lat8[...]) + shifted
        local[j, 8:16] = held[8:16]
        return carry

    lax.fori_loop(0, rows, settle, 0, unroll=8)

    def ghosts(i, carry):
        for c, out in zip(DIRS, outs):
            out[i] = local[jnp.maximum(send[c, i], 0)]
        return carry

    lax.fori_loop(0, outs[0].shape[0], ghosts, 0)


def apply_kernel(first, pairs, order, bounds, send, spread, words, local, *rest):
    ghosts, rest = rest[:8], rest[8:]
    if not first:
        field, field_ghosts, rest = rest[0], rest[1:9], rest[9:]
    image, rest = rest[0], rest[1:]
    if first:
        sends, rest = rest[:8], rest[8:]
    full, turned, total = rest
    rows, _, points = local.shape
    cap = ghosts[0].shape[0]
    full[0:rows] = local[...]
    full[rows + 4 * cap : rows + 5 * cap] = jnp.zeros((cap,) + full.shape[1:], F32)
    for e, ghost in zip(DIRS, ghosts):
        full[rows + e * cap : rows + (e + 1) * cap] = ghost[...]
    if not first:
        full[0:rows, 8:11, :] = field[...]
        for e, ghost in zip(DIRS, field_ghosts):
            full[rows + e * cap : rows + (e + 1) * cap, 8:16, :] = ghost[...]

    def turn(j, carry):
        state = full[j]
        high = state.astype(jnp.bfloat16).astype(F32)
        rest_of = state - high
        middle = rest_of.astype(jnp.bfloat16).astype(F32)
        turned[j] = jnp.transpose(jnp.concatenate([high, middle, rest_of - middle], axis=0))
        return carry

    lax.fori_loop(0, full.shape[0], turn, 0, unroll=8)
    total[...] = jnp.zeros_like(total)

    def bonds(side_b, side_a, flags, acc, guard):
        part = lambda c: side_b[FIELDS.index(c)]
        xi = [part(c) - side_a[c] for c in range(3)]
        y = [part(3 + c) - side_a[3 + c] for c in range(3)]
        dv = [part(8 + c) - side_a[8 + c] for c in range(3)]
        r2 = xi[0] * xi[0] + xi[1] * xi[1] + xi[2] * xi[2]
        l2 = y[0] * y[0] + y[1] * y[1] + y[2] * y[2]
        weight = jnp.maximum(1.0 - r2 * (1.0 / 9.0), 0.0)
        c = (part(6) + side_a[6]) * jnp.where(flags == 0, weight, 0.0)
        if guard:
            c = jnp.where(r2 < 1e-2, 0.0, c)
            r2 = jnp.maximum(r2, 1e-2)
            l2 = jnp.maximum(l2, 1e-2)
        r_inv = lax.rsqrt(r2)
        l_inv = lax.rsqrt(l2)
        cl = c * l_inv
        k2 = c * r_inv - cl
        along = cl * (l_inv * l_inv) * (y[0] * dv[0] + y[1] * dv[1] + y[2] * dv[2])
        return [acc[i] + (k2 * dv[i] + along * y[i]) for i in range(3)]

    def pair(kind, slot):
        live = slot >= 0
        q = jnp.maximum(slot, 0)
        tile = pairs[0, q]
        partner = pairs[1, q]
        sx = pairs[2, q]
        sy = pairs[3, q]
        dx = (sx * 8).astype(F32)
        dy = (sy * (points // 16)).astype(F32)
        side_a = []
        for c in range(11):
            if c == 7:
                side_a.append(None)
                continue
            row = full[tile, c : c + 1]
            if c in (0, 3) and kind & 1:
                row = row - dx
            if c in (1, 4) and kind & 2:
                row = row - dy
            side_a.append(jnp.broadcast_to(row, (8, points)))
        blocks, words_of = [], []
        x0 = jnp.where(sx > 0, 0, 5) if kind & 1 else 0
        if kind < 2:
            for k in range(3 if kind else 8):
                for z in range(2):
                    block = turned[partner, pl.ds(x0 + k + 64 * z, 8, stride=8), :]
                    flags = words[q, 8 * z : 8 * z + 8] & jnp.left_shift(1, x0 + k)
                    blocks.append(block)
                    words_of.append(flags)
        elif kind == 2:
            y0 = jnp.where(sy > 0, 0, 5)
            bit = jnp.left_shift(1, lax.broadcasted_iota(jnp.int32, (8, points), 0))
            for k in range(3):
                for z in range(2):
                    start = (y0 + k) * 8 + 64 * z
                    block = turned[partner, pl.ds(pl.multiple_of(start, 8), 8), :]
                    word = jnp.broadcast_to(words[q, pl.ds(y0 + k + 8 * z, 1), :], (8, points))
                    blocks.append(block)
                    words_of.append(word & bit)
        else:
            y0 = jnp.where(sy > 0, 0, 4)
            word = jnp.concatenate([words[q, pl.ds(y0, 4), :], words[q, pl.ds(y0 + 8, 4), :]], axis=0)
            for k in range(3):
                start = x0 + k + 8 * y0
                block = jnp.concatenate(
                    [
                        turned[partner, pl.ds(start, 4, stride=8), :],
                        turned[partner, pl.ds(start + 64, 4, stride=8), :],
                    ],
                    axis=0,
                )
                blocks.append(block)
                words_of.append(word & jnp.left_shift(1, x0 + k))
        return live, tile, side_a, blocks, words_of

    for kind, width in enumerate(UNROLL):

        def step(i, carry, kind=kind, width=width):
            batch = [pair(kind, order[i * width + u]) for u in range(width)]
            stacked = jnp.concatenate([b for one in batch for b in one[3]], axis=0)
            wide = jnp.dot(stacked.astype(jnp.bfloat16), spread[...], preferred_element_type=F32)
            at = 0
            done = []
            for live, tile, side_a, blocks, words_of in batch:
                acc = [jnp.zeros((8, points), F32)] * 3
                for flags in words_of:
                    side_b = [wide[at : at + 8, n * points : (n + 1) * points] for n in range(len(FIELDS))]
                    acc = bonds(side_b, side_a, flags, acc, kind == 0)
                    at += 8
                done.append((tile, [jnp.where(live, term, 0.0) for term in acc]))
            for tile, acc in done:
                for c in range(3):
                    total[tile, c] += acc[c]
            return carry

        lax.fori_loop(bounds[2 * kind], bounds[2 * kind + 1], step, 0)

    def close(j, carry):
        image[j] = jnp.sum(total[j], axis=1)
        return carry

    lax.fori_loop(0, rows, close, 0, unroll=4)
    if first:
        for out in sends:
            out[...] = jnp.zeros_like(out)

        def ghost_rows(i, carry):
            for c, out in zip(DIRS, sends):
                out[i, 0:3] = image[jnp.maximum(send[c, i], 0)]
            return carry

        lax.fori_loop(0, cap, ghost_rows, 0)


def exchange_kernel(offsets, *refs):
    n = len(offsets)
    ins, outs, send_sem, recv_sem = refs[:n], refs[n : 2 * n], refs[2 * n], refs[2 * n + 1]
    n_x, n_y = lax.axis_size("gx"), lax.axis_size("gy")
    x, y = lax.axis_index("gx"), lax.axis_index("gy")

    def exists(ox, oy):
        return (x + ox >= 0) & (x + ox < n_x) & (y + oy >= 0) & (y + oy < n_y)

    barrier = pltpu.get_barrier_semaphore()
    for ox, oy in offsets:

        @pl.when(exists(ox, oy))
        def _():
            pl.semaphore_signal(
                barrier, inc=1, device_id=(x + ox, y + oy), device_id_type=pl.DeviceIdType.MESH
            )

    peers = sum(jnp.where(exists(ox, oy), 1, 0) for ox, oy in offsets)
    pl.semaphore_wait(barrier, peers)

    def copy(d):
        ox, oy = offsets[d]
        back = offsets.index((-ox, -oy))
        return pltpu.make_async_remote_copy(
            src_ref=ins[d],
            dst_ref=outs[back],
            send_sem=send_sem.at[d],
            recv_sem=recv_sem.at[back],
            device_id=(x + ox, y + oy),
            device_id_type=pl.DeviceIdType.MESH,
        )

    for d, (ox, oy) in enumerate(offsets):

        @pl.when(exists(ox, oy))
        def _():
            copy(d).start()

        @pl.when(jnp.logical_not(exists(ox, oy)))
        def _():
            outs[d][...] = jnp.zeros_like(outs[d])

    for d, (ox, oy) in enumerate(offsets):

        @pl.when(exists(ox, oy))
        def _():
            copy(d).wait_send()
            copy(offsets.index((-ox, -oy))).wait_recv()


def exchange(blocks, offsets, ident):
    n = len(offsets)
    return pl.pallas_call(
        functools.partial(exchange_kernel, offsets),
        out_shape=[jax.ShapeDtypeStruct(b.shape, b.dtype) for b in blocks],
        in_specs=[VMEM] * n,
        out_specs=[VMEM] * n,
        scratch_shapes=[pltpu.SemaphoreType.DMA((n,)), pltpu.SemaphoreType.DMA((n,))],
        compiler_params=pltpu.CompilerParams(
            collective_id=ident, has_side_effects=True, vmem_limit_bytes=16 * 1024 * 1024
        ),
    )(*blocks)


SIDES = ((-1, 0), (1, 0), (0, -1), (0, 1))
AROUND = tuple((e // 3 - 1, e % 3 - 1) for e in DIRS)
UNROLL = (2, 8, 8, 16)


def by_kind(pair_list, count):
    pairs = pair_list.shape[1]
    slot = jnp.arange(pairs, dtype=jnp.int32)
    kind = (pair_list[2] != 0).astype(jnp.int32) + 2 * (pair_list[3] != 0).astype(jnp.int32)
    kind = jnp.where(slot < count, kind, 4)
    earlier = (kind[:, None] == kind[None, :]) & (slot[:, None] < slot[None, :])
    place = jnp.sum(earlier.astype(jnp.int32), axis=0)
    start, bounds = jnp.int32(0), []
    for k, width in enumerate(UNROLL):
        members = jnp.sum((kind == k).astype(jnp.int32))
        place = place + jnp.where(kind == k, start, 0)
        bounds += [start // width, (start + members + width - 1) // width]
        start = start + (members + 15) // 16 * 16
    place = jnp.where(kind < 4, place, -1)
    hit = place[:, None] == jnp.arange(pairs + 64, dtype=jnp.int32)[None, :]
    order = jnp.sum(jnp.where(hit, slot[:, None] + 1, 0), axis=0) - 1
    return order, jnp.stack(bounds)


def on_device(jitter, displacement, modulus, start_vec, old_home, ghost_send, pair_list, pair_count, broken):
    tiles = old_home.shape[0]
    points = jitter.shape[2]
    cap = ghost_send.shape[2]
    width_y = lax.axis_size("gy")
    anchor = old_home // tiles
    old_slot = old_home % tiles
    off_x = anchor // width_y - lax.axis_index("gx")
    off_y = anchor % width_y - lax.axis_index("gy")
    side = jnp.where(off_x == -1, 0, jnp.where(off_x == 1, 1, jnp.where(off_y == -1, 2, jnp.where(off_y == 1, 3, 4))))
    index = jnp.arange(tiles, dtype=jnp.int32)
    earlier = (side[:, None] == side[None, :]) & (index[:, None] < index[None, :])
    ranked = jnp.sum(earlier.astype(jnp.int32), axis=0)
    cell = jnp.where(side < 4, side * CAP + ranked, -1)
    hit = cell[:, None] == jnp.arange(4 * CAP, dtype=jnp.int32)[None, :]
    wanted = jnp.sum(jnp.where(hit, old_slot[:, None], 0), axis=0).reshape(4, CAP)
    requests = [jnp.pad(wanted[d : d + 1], ((0, 7), (0, 128 - CAP))) for d in range(4)]
    asked = jnp.concatenate([r[0:1] for r in exchange(requests, SIDES, 0)], axis=0)
    pick = jnp.where(side < 4, tiles + cell, old_slot)

    state = (jitter, displacement, modulus, start_vec)
    handed = pl.pallas_call(
        hand_kernel,
        out_shape=[jax.ShapeDtypeStruct((CAP, 16, points), F32)] * 4,
        in_specs=[SMEM] + [VMEM] * 4,
        out_specs=[VMEM] * 4,
        compiler_params=LIMIT,
    )(asked, *state)
    arrived = exchange(handed, SIDES, 1)
    lat = lattice(points)
    lat8 = jnp.concatenate([lat, jnp.zeros((5, points), F32)], axis=0)
    ghost_shape = jax.ShapeDtypeStruct((cap, 16, points), F32)
    local, *sends = pl.pallas_call(
        settle_kernel,
        out_shape=[jax.ShapeDtypeStruct((tiles, 16, points), F32)] + [ghost_shape] * 8,
        in_specs=[SMEM] * 2 + [VMEM] * 9,
        out_specs=[VMEM] * 9,
        scratch_shapes=[pltpu.VMEM((tiles + 4 * CAP, 16, points), F32)],
        compiler_params=LIMIT,
    )(pick, ghost_send[0], lat8, *state, *arrived)
    ghosts = exchange(sends, AROUND, 2)
    rows = tiles + 9 * cap
    scratch = [
        pltpu.VMEM((rows, 16, points), F32),
        pltpu.VMEM((rows, points, 48), F32),
        pltpu.VMEM((tiles, 3, 8, points), F32),
    ]
    image_shape = jax.ShapeDtypeStruct((tiles, 3, points), F32)
    order, bounds = by_kind(pair_list[0], pair_count[0])
    row = jnp.arange(48, dtype=jnp.int32)[:, None] % 16
    field = jnp.repeat(jnp.array(FIELDS, jnp.int32), points)[None, :]
    spread = (row == field).astype(jnp.bfloat16)
    head = (pair_list[0], order, bounds, ghost_send[0], spread, broken, local, *ghosts)
    first_image, *image_sends = pl.pallas_call(
        functools.partial(apply_kernel, True),
        out_shape=[image_shape] + [jax.ShapeDtypeStruct((cap, 8, points), F32)] * 8,
        in_specs=[SMEM] * 4 + [VMEM] * 11,
        out_specs=[VMEM] * 9,
        scratch_shapes=scratch,
        compiler_params=LIMIT,
    )(*head)
    image_ghosts = exchange(image_sends, AROUND, 3)
    second_image = pl.pallas_call(
        functools.partial(apply_kernel, False),
        out_shape=image_shape,
        in_specs=[SMEM] * 4 + [VMEM] * 20,
        out_specs=VMEM,
        scratch_shapes=scratch,
        compiler_params=LIMIT,
    )(*head, first_image, *image_ghosts)
    return (first_image, second_image)


def solution(mesh):
    split = ("gx", "gy")
    spec3, spec2, spec1 = P(split, None, None), P(split, None), P(split)
    return jax.shard_map(
        on_device,
        mesh=mesh,
        in_specs=(spec3, spec3, spec2, spec3, spec1, spec3, spec3, spec1, spec3),
        out_specs=(spec3, spec3),
        check_vma=False,
    )
```

```python
import functools
import jax
import jax.numpy as jnp
from jax import lax
from jax.experimental import pallas as pl
from jax.experimental.pallas import tpu as pltpu
from jax.sharding import PartitionSpec as P

CAP = 16
F32 = jnp.float32
VMEM = pl.BlockSpec(memory_space=pltpu.VMEM)
SMEM = pl.BlockSpec(memory_space=pltpu.SMEM)
LIMIT = pltpu.CompilerParams(vmem_limit_bytes=48 * 1024 * 1024)
DIRS = (0, 1, 2, 3, 5, 6, 7, 8)
FIELDS = (0, 1, 2, 3, 4, 5, 6, 8, 9, 10)


def lattice(points):
    counter = jnp.arange(points, dtype=jnp.int32)
    return jnp.stack([counter % 8, counter // 8 % (points // 16), counter // (points // 2)]).astype(F32)


def hand_kernel(asked, jit, disp, mod, vec, *outs):
    for out in outs:
        out[...] = jnp.zeros_like(out)

    def body(i, carry):
        for d, out in enumerate(outs):
            row = asked[d, i]
            out[i, 0:3] = jit[row]
            out[i, 3:6] = disp[row]
            out[i, 6:7] = mod[pl.ds(row, 1)]
            out[i, 8:11] = vec[row]
        return carry

    lax.fori_loop(0, CAP, body, 0)


def settle_kernel(pick, send, lat8, jit, disp, mod, vec, in0, in1, in2, in3, local, *rest):
    outs, pool = rest[:8], rest[8]
    rows = jit.shape[0]
    pool[0:rows] = jnp.zeros((rows,) + pool.shape[1:], F32)
    pool[0:rows, 0:3, :] = jit[...]
    pool[0:rows, 3:6, :] = disp[...]
    pool[0:rows, 8:11, :] = vec[...]

    def put_mod(j, carry):
        pool[j, 6:7, :] = mod[pl.ds(j, 1)]
        return carry

    lax.fori_loop(0, rows, put_mod, 0, unroll=8)
    for d, arrived in enumerate((in0, in1, in2, in3)):
        pool[rows + d * CAP : rows + (d + 1) * CAP] = arrived[...]
    points = jit.shape[2]
    sub = lax.broadcasted_iota(jnp.int32, (8, points), 0)
    scale = jnp.where(sub == 6, 0.05, 1.0)
    moved = (sub >= 3) & (sub < 6)

    def settle(j, carry):
        held = pool[pick[j]]
        low = held[0:8]
        base = low + lat8[...]
        shifted = jnp.where(moved, pltpu.roll(base, 3, 0), 0.0)
        local[j, 0:8] = low * scale + jnp.where(moved, 0.0, lat8[...]) + shifted
        local[j, 8:16] = held[8:16]
        return carry

    lax.fori_loop(0, rows, settle, 0, unroll=8)

    def ghosts(i, carry):
        for c, out in zip(DIRS, outs):
            out[i] = local[jnp.maximum(send[c, i], 0)]
        return carry

    lax.fori_loop(0, outs[0].shape[0], ghosts, 0)


def apply_kernel(first, pairs, order, bounds, send, spread, words, local, *rest):
    ghosts, rest = rest[:8], rest[8:]
    if not first:
        field, field_ghosts, rest = rest[0], rest[1:9], rest[9:]
    image, rest = rest[0], rest[1:]
    if first:
        sends, rest = rest[:8], rest[8:]
    full, turned, total = rest
    rows, _, points = local.shape
    cap = ghosts[0].shape[0]
    full[0:rows] = local[...]
    full[rows + 4 * cap : rows + 5 * cap] = jnp.zeros((cap,) + full.shape[1:], F32)
    for e, ghost in zip(DIRS, ghosts):
        full[rows + e * cap : rows + (e + 1) * cap] = ghost[...]
    if not first:
        full[0:rows, 8:11, :] = field[...]
        for e, ghost in zip(DIRS, field_ghosts):
            full[rows + e * cap : rows + (e + 1) * cap, 8:16, :] = ghost[...]

    def turn(j, carry):
        state = full[j]
        high = state.astype(jnp.bfloat16).astype(F32)
        rest_of = state - high
        middle = rest_of.astype(jnp.bfloat16).astype(F32)
        turned[j] = jnp.transpose(jnp.concatenate([high, middle, rest_of - middle], axis=0))
        return carry

    lax.fori_loop(0, full.shape[0], turn, 0, unroll=8)
    total[...] = jnp.zeros_like(total)

    def bonds(side_b, side_a, flags, acc, guard):
        part = lambda c: side_b[FIELDS.index(c)]
        xi = [part(c) - side_a[c] for c in range(3)]
        y = [part(3 + c) - side_a[3 + c] for c in range(3)]
        dv = [part(8 + c) - side_a[8 + c] for c in range(3)]
        r2 = xi[0] * xi[0] + xi[1] * xi[1] + xi[2] * xi[2]
        l2 = y[0] * y[0] + y[1] * y[1] + y[2] * y[2]
        weight = jnp.maximum(1.0 - r2 * (1.0 / 9.0), 0.0)
        c = (part(6) + side_a[6]) * jnp.where(flags == 0, weight, 0.0)
        if guard:
            c = jnp.where(r2 < 1e-2, 0.0, c)
            r2 = jnp.maximum(r2, 1e-2)
            l2 = jnp.maximum(l2, 1e-2)
        r_inv = lax.rsqrt(r2)
        l_inv = lax.rsqrt(l2)
        cl = c * l_inv
        k2 = c * r_inv - cl
        along = cl * (l_inv * l_inv) * (y[0] * dv[0] + y[1] * dv[1] + y[2] * dv[2])
        return [acc[i] + (k2 * dv[i] + along * y[i]) for i in range(3)]

    def pair(kind, slot):
        live = slot >= 0
        q = jnp.maximum(slot, 0)
        tile = pairs[0, q]
        partner = pairs[1, q]
        sx = pairs[2, q]
        sy = pairs[3, q]
        dx = (sx * 8).astype(F32)
        dy = (sy * (points // 16)).astype(F32)
        side_a = []
        for c in range(11):
            if c == 7:
                side_a.append(None)
                continue
            row = full[tile, c : c + 1]
            if c in (0, 3) and kind & 1:
                row = row - dx
            if c in (1, 4) and kind & 2:
                row = row - dy
            side_a.append(jnp.broadcast_to(row, (8, points)))
        blocks, words_of = [], []
        x0 = jnp.where(sx > 0, 0, 5) if kind & 1 else 0
        if kind < 2:
            for k in range(3 if kind else 8):
                for z in range(2):
                    block = turned[partner, pl.ds(x0 + k + 64 * z, 8, stride=8), :]
                    flags = words[q, 8 * z : 8 * z + 8] & jnp.left_shift(1, x0 + k)
                    blocks.append(block)
                    words_of.append(flags)
        elif kind == 2:
            y0 = jnp.where(sy > 0, 0, 5)
            bit = jnp.left_shift(1, lax.broadcasted_iota(jnp.int32, (8, points), 0))
            for k in range(3):
                for z in range(2):
                    start = (y0 + k) * 8 + 64 * z
                    block = turned[partner, pl.ds(pl.multiple_of(start, 8), 8), :]
                    word = jnp.broadcast_to(words[q, pl.ds(y0 + k + 8 * z, 1), :], (8, points))
                    blocks.append(block)
                    words_of.append(word & bit)
        else:
            y0 = jnp.where(sy > 0, 0, 4)
            word = jnp.concatenate([words[q, pl.ds(y0, 4), :], words[q, pl.ds(y0 + 8, 4), :]], axis=0)
            for k in range(3):
                start = x0 + k + 8 * y0
                block = jnp.concatenate(
                    [
                        turned[partner, pl.ds(start, 4, stride=8), :],
                        turned[partner, pl.ds(start + 64, 4, stride=8), :],
                    ],
                    axis=0,
                )
                blocks.append(block)
                words_of.append(word & jnp.left_shift(1, x0 + k))
        return live, tile, side_a, blocks, words_of

    for kind, width in enumerate(UNROLL):

        def step(i, carry, kind=kind, width=width):
            batch = [pair(kind, order[i * width + u]) for u in range(width)]
            stacked = jnp.concatenate([b for one in batch for b in one[3]], axis=0)
            wide = jnp.dot(stacked.astype(jnp.bfloat16), spread[...], preferred_element_type=F32)
            at = 0
            done = []
            for live, tile, side_a, blocks, words_of in batch:
                acc = [jnp.zeros((8, points), F32)] * 3
                for flags in words_of:
                    side_b = [wide[at : at + 8, n * points : (n + 1) * points] for n in range(len(FIELDS))]
                    acc = bonds(side_b, side_a, flags, acc, kind == 0)
                    at += 8
                done.append((tile, [jnp.where(live, term, 0.0) for term in acc]))
            for tile, acc in done:
                for c in range(3):
                    total[tile, c] += acc[c]
            return carry

        lax.fori_loop(bounds[2 * kind], bounds[2 * kind + 1], step, 0)

    def close(j, carry):
        image[j] = jnp.sum(total[j], axis=1)
        return carry

    lax.fori_loop(0, rows, close, 0, unroll=4)
    if first:
        for out in sends:
            out[...] = jnp.zeros_like(out)

        def ghost_rows(i, carry):
            for c, out in zip(DIRS, sends):
                out[i, 0:3] = image[jnp.maximum(send[c, i], 0)]
            return carry

        lax.fori_loop(0, cap, ghost_rows, 0)


def exchange_kernel(offsets, *refs):
    n = len(offsets)
    ins, outs, send_sem, recv_sem = refs[:n], refs[n : 2 * n], refs[2 * n], refs[2 * n + 1]
    n_x, n_y = lax.axis_size("gx"), lax.axis_size("gy")
    x, y = lax.axis_index("gx"), lax.axis_index("gy")

    def exists(ox, oy):
        return (x + ox >= 0) & (x + ox < n_x) & (y + oy >= 0) & (y + oy < n_y)

    barrier = pltpu.get_barrier_semaphore()
    for ox, oy in offsets:

        @pl.when(exists(ox, oy))
        def _():
            pl.semaphore_signal(
                barrier, inc=1, device_id=(x + ox, y + oy), device_id_type=pl.DeviceIdType.MESH
            )

    peers = sum(jnp.where(exists(ox, oy), 1, 0) for ox, oy in offsets)
    pl.semaphore_wait(barrier, peers)

    def copy(d):
        ox, oy = offsets[d]
        back = offsets.index((-ox, -oy))
        return pltpu.make_async_remote_copy(
            src_ref=ins[d],
            dst_ref=outs[back],
            send_sem=send_sem.at[d],
            recv_sem=recv_sem.at[back],
            device_id=(x + ox, y + oy),
            device_id_type=pl.DeviceIdType.MESH,
        )

    for d, (ox, oy) in enumerate(offsets):

        @pl.when(exists(ox, oy))
        def _():
            copy(d).start()

        @pl.when(jnp.logical_not(exists(ox, oy)))
        def _():
            outs[d][...] = jnp.zeros_like(outs[d])

    for d, (ox, oy) in enumerate(offsets):

        @pl.when(exists(ox, oy))
        def _():
            copy(d).wait_send()
            copy(offsets.index((-ox, -oy))).wait_recv()


def exchange(blocks, offsets, ident):
    n = len(offsets)
    return pl.pallas_call(
        functools.partial(exchange_kernel, offsets),
        out_shape=[jax.ShapeDtypeStruct(b.shape, b.dtype) for b in blocks],
        in_specs=[VMEM] * n,
        out_specs=[VMEM] * n,
        scratch_shapes=[pltpu.SemaphoreType.DMA((n,)), pltpu.SemaphoreType.DMA((n,))],
        compiler_params=pltpu.CompilerParams(
            collective_id=ident, has_side_effects=True, vmem_limit_bytes=16 * 1024 * 1024
        ),
    )(*blocks)


SIDES = ((-1, 0), (1, 0), (0, -1), (0, 1))
AROUND = tuple((e // 3 - 1, e % 3 - 1) for e in DIRS)
UNROLL = (4, 8, 8, 16)


def by_kind(pair_list, count):
    pairs = pair_list.shape[1]
    slot = jnp.arange(pairs, dtype=jnp.int32)
    kind = (pair_list[2] != 0).astype(jnp.int32) + 2 * (pair_list[3] != 0).astype(jnp.int32)
    kind = jnp.where(slot < count, kind, 4)
    earlier = (kind[:, None] == kind[None, :]) & (slot[:, None] < slot[None, :])
    place = jnp.sum(earlier.astype(jnp.int32), axis=0)
    start, bounds = jnp.int32(0), []
    for k, width in enumerate(UNROLL):
        members = jnp.sum((kind == k).astype(jnp.int32))
        place = place + jnp.where(kind == k, start, 0)
        bounds += [start // width, (start + members + width - 1) // width]
        start = start + (members + 15) // 16 * 16
    place = jnp.where(kind < 4, place, -1)
    hit = place[:, None] == jnp.arange(pairs + 64, dtype=jnp.int32)[None, :]
    order = jnp.sum(jnp.where(hit, slot[:, None] + 1, 0), axis=0) - 1
    return order, jnp.stack(bounds)


def on_device(jitter, displacement, modulus, start_vec, old_home, ghost_send, pair_list, pair_count, broken):
    tiles = old_home.shape[0]
    points = jitter.shape[2]
    cap = ghost_send.shape[2]
    width_y = lax.axis_size("gy")
    anchor = old_home // tiles
    old_slot = old_home % tiles
    off_x = anchor // width_y - lax.axis_index("gx")
    off_y = anchor % width_y - lax.axis_index("gy")
    side = jnp.where(off_x == -1, 0, jnp.where(off_x == 1, 1, jnp.where(off_y == -1, 2, jnp.where(off_y == 1, 3, 4))))
    index = jnp.arange(tiles, dtype=jnp.int32)
    earlier = (side[:, None] == side[None, :]) & (index[:, None] < index[None, :])
    ranked = jnp.sum(earlier.astype(jnp.int32), axis=0)
    cell = jnp.where(side < 4, side * CAP + ranked, -1)
    hit = cell[:, None] == jnp.arange(4 * CAP, dtype=jnp.int32)[None, :]
    wanted = jnp.sum(jnp.where(hit, old_slot[:, None], 0), axis=0).reshape(4, CAP)
    requests = [jnp.pad(wanted[d : d + 1], ((0, 7), (0, 128 - CAP))) for d in range(4)]
    asked = jnp.concatenate([r[0:1] for r in exchange(requests, SIDES, 0)], axis=0)
    pick = jnp.where(side < 4, tiles + cell, old_slot)

    state = (jitter, displacement, modulus, start_vec)
    handed = pl.pallas_call(
        hand_kernel,
        out_shape=[jax.ShapeDtypeStruct((CAP, 16, points), F32)] * 4,
        in_specs=[SMEM] + [VMEM] * 4,
        out_specs=[VMEM] * 4,
        compiler_params=LIMIT,
    )(asked, *state)
    arrived = exchange(handed, SIDES, 1)
    lat = lattice(points)
    lat8 = jnp.concatenate([lat, jnp.zeros((5, points), F32)], axis=0)
    ghost_shape = jax.ShapeDtypeStruct((cap, 16, points), F32)
    local, *sends = pl.pallas_call(
        settle_kernel,
        out_shape=[jax.ShapeDtypeStruct((tiles, 16, points), F32)] + [ghost_shape] * 8,
        in_specs=[SMEM] * 2 + [VMEM] * 9,
        out_specs=[VMEM] * 9,
        scratch_shapes=[pltpu.VMEM((tiles + 4 * CAP, 16, points), F32)],
        compiler_params=LIMIT,
    )(pick, ghost_send[0], lat8, *state, *arrived)
    ghosts = exchange(sends, AROUND, 2)
    rows = tiles + 9 * cap
    scratch = [
        pltpu.VMEM((rows, 16, points), F32),
        pltpu.VMEM((rows, points, 48), F32),
        pltpu.VMEM((tiles, 3, 8, points), F32),
    ]
    image_shape = jax.ShapeDtypeStruct((tiles, 3, points), F32)
    order, bounds = by_kind(pair_list[0], pair_count[0])
    row = jnp.arange(48, dtype=jnp.int32)[:, None] % 16
    field = jnp.repeat(jnp.array(FIELDS, jnp.int32), points)[None, :]
    spread = (row == field).astype(jnp.bfloat16)
    head = (pair_list[0], order, bounds, ghost_send[0], spread, broken, local, *ghosts)
    first_image, *image_sends = pl.pallas_call(
        functools.partial(apply_kernel, True),
        out_shape=[image_shape] + [jax.ShapeDtypeStruct((cap, 8, points), F32)] * 8,
        in_specs=[SMEM] * 4 + [VMEM] * 11,
        out_specs=[VMEM] * 9,
        scratch_shapes=scratch,
        compiler_params=LIMIT,
    )(*head)
    image_ghosts = exchange(image_sends, AROUND, 3)
    second_image = pl.pallas_call(
        functools.partial(apply_kernel, False),
        out_shape=image_shape,
        in_specs=[SMEM] * 4 + [VMEM] * 20,
        out_specs=VMEM,
        scratch_shapes=scratch,
        compiler_params=LIMIT,
    )(*head, first_image, *image_ghosts)
    return (first_image, second_image)


def solution(mesh):
    split = ("gx", "gy")
    spec3, spec2, spec1 = P(split, None, None), P(split, None), P(split)
    return jax.shard_map(
        on_device,
        mesh=mesh,
        in_specs=(spec3, spec3, spec2, spec3, spec1, spec3, spec3, spec1, spec3),
        out_specs=(spec3, spec3),
        check_vma=False,
    )
```
